32 devices in a mesh: group: 2 (over y), expert: 16 (over z, x, core).
Axes of the slice: x: 2, y: 2, z: 4, core: 2. Of those that a mesh axis runs over, the one named last changes fastest.
Arguments:
- tokens: bfloat16 [2048, 3072], P(('group', 'expert')), parts along dimension 0, may hold values from -6 to 6
- expert_ids: int32 [2048, 4], P(('group', 'expert')), parts along dimension 0, may hold values from 0 to 15, all different within a row; in each aligned block of 64 rows (0 to 63, 64 to 127, ...) at most 18 rows name the same one
- gate_fixed: int32 [2048, 4], P(('group', 'expert')), parts along dimension 0, may hold values from 1 to 65535
- gate_q: bfloat16 [3072, 43008], P(None, 'expert'), may hold values from -127 to 127
- up_q: bfloat16 [3072, 43008], P(None, 'expert'), may hold values from -127 to 127
- down_q: bfloat16 [43008, 3072], P('expert'), may hold values from -127 to 127
- gate_scale: float32 [43008], P('expert'), as said below
- up_scale: float32 [43008], P('expert'), as said below
- down_scale: float32 [8, 3072], replicated, as said below
Outputs:
- mixed: bfloat16 [2048, 3072], P(('group', 'expert')), parts along dimension 0
The draws below stay inside these ranges and needn't reach their ends.
There are 2 independent parts, one for each index of `group`. The reference program is written for one: setup_inputs(seed, part) draws one part's arguments, and reference() takes and returns one part's arrays. A program takes and returns all parts, laid end to end along the dimension named above; an argument that names none is the same for every part. Nothing has to cross between parts.
Inputs may be any that keep to these rules, and one draw needn't show every extreme that they name: `expert_ids`: each row names 4 different experts; among the 64 rows of one device at most 18 name one expert, and some device reaches 18. `gate_scale`: Positive. `up_scale`: Positive. `down_scale`: Positive.
All inputs are finite; a program needn't handle non-finite values.
Results may differ from the reference program's by a relative error of at most 0.0085.
Values may be sent and summed in bfloat16 or wider, within the bound.
A program may use at most 128 MiB of HBM per device.

```python
import math
import jax
import jax.numpy as jnp
import numpy as np
from jax import lax

D = 3072
FF = 5376
EXPERTS = 16
WINDOW = 8
TOP = 4
TOK_DEV = 64
CAP = 18
TOKENS = 1024
N_EXPERT = 16


def draw_gate_q(key, part):
    key = jax.random.fold_in(key, 11)
    return jax.random.randint(key, (D, WINDOW * FF), -127, 128).astype(jnp.float32).astype(jnp.bfloat16)


def draw_up_q(key, part):
    key = jax.random.fold_in(key, 12)
    return jax.random.randint(key, (D, WINDOW * FF), -127, 128).astype(jnp.float32).astype(jnp.bfloat16)


def draw_down_q(key, part):
    key = jax.random.fold_in(key, 13)
    return jax.random.randint(key, (WINDOW * FF, D), -127, 128).astype(jnp.float32).astype(jnp.bfloat16)


def spread_scale(key, shape, fan_in):
    spread = jax.random.uniform(key, shape, jnp.float32, math.log(0.5), math.log(2.0))
    return jnp.exp(spread) / (73.6 * math.sqrt(fan_in))


def draw_gate_scale(key, part):
    key = jax.random.fold_in(key, 14)
    return spread_scale(key, (WINDOW * FF,), D)


def draw_up_scale(key, part):
    key = jax.random.fold_in(key, 15)
    return spread_scale(key, (WINDOW * FF,), D)


def draw_down_scale(key, part):
    key = jax.random.fold_in(key, 16)
    return spread_scale(key, (WINDOW, D), FF)


def place_ends(drawn, rng, least, largest):
    extent = drawn.shape
    place = [jax.random.randint(jax.random.fold_in(rng, axis), (), 0, extent[axis]) for axis in range(len(extent))]
    drawn = drawn.at[tuple(place)].set(least)
    longest = extent.index(max(extent))
    place[longest] = (place[longest] + 1) % extent[longest]
    return drawn.at[tuple(place)].set(largest)


def shard_levels(rng, dims, shards, least, largest):
    gain = 1.0
    for axis_at, shards_of in shards:
        heights = jax.random.uniform(jax.random.fold_in(jax.random.fold_in(rng, 6), axis_at), (shards_of,), jnp.float32, least / len(shards), largest / len(shards))
        gain = gain * jnp.repeat(jnp.exp(heights), dims[axis_at] // shards_of).reshape((-1,) + (1,) * (len(dims) - 1 - axis_at))
    return gain


def deal_out(stream_key, own, number, rows, amount, top, bound, lean):
    order = jax.random.permutation(stream_key, amount)
    heavy_load, common = portions_of(amount, rows * top, bound, lean, True), portions_of(amount, rows * top, bound, lean, False)
    places = jnp.arange(amount)

    def named(tallies, turn):
        used = int((tallies > 0).sum())
        fixed = max(1, used // 4)
        shifted = fixed + (places - fixed + turn * (used - fixed)) % max(1, amount - fixed)
        return jnp.zeros((amount,), jnp.int32).at[order[jnp.where(places < fixed, places, shifted)]].set(jnp.asarray(tallies, jnp.int32))

    tallies = jnp.where(number % 4 == 0, named(heavy_load, number // 4), named(common, number - number // 4 - 1))
    mixed = jax.random.permutation(jax.random.fold_in(own, 3), amount)
    source_of, taker = mixed[0:amount // 2 * 2:2], mixed[1:amount // 2 * 2:2]
    margin = jnp.minimum(tallies[source_of] - 1, bound - tallies[taker]) // 2
    margin = jnp.where((source_of == order[0]) | (taker == order[0]) | (tallies[taker] == 0), 0, jnp.maximum(margin, 0))
    shifted = jax.random.randint(jax.random.fold_in(own, 4), (amount // 2,), 0, 1 << 20) % (margin + 1)
    tallies = tallies.at[source_of].add(-shifted).at[taker].add(shifted)
    labels = jnp.searchsorted(jnp.cumsum(tallies), jnp.arange(rows * top), side="right").astype(jnp.int32)
    table = labels.reshape(top, rows).T
    table = table[jax.random.permutation(jax.random.fold_in(own, 1), rows)]
    turn = jax.random.randint(jax.random.fold_in(own, 2), (rows, 1), 0, top)
    return jnp.take_along_axis(table, (jnp.arange(top)[None, :] + turn) % top, axis=1)


def portions_of(number_of, total, bound, skew, full):
    loads = [(1 << 20) // math.isqrt(standing ** skew) + 1 for standing in range(1, number_of + 1)]
    largest = bound if full else min(bound, max(-(-total // number_of), total * loads[0] // sum(loads)))
    least = 1 if total - largest >= number_of - 1 else 0
    holding, rest = [largest] + [least] * (number_of - 1), total - largest - least * (number_of - 1)
    while rest > 0:
        candidates = [i for i in range(1, number_of) if holding[i] < largest] or [i for i in range(1, number_of) if holding[i] < bound]
        pool, remaining = sum([loads[i] for i in candidates]), rest
        for i in candidates:
            extra = min(bound - holding[i], max(1, remaining * loads[i] // pool), rest)
            holding[i] = holding[i] + extra
            rest = rest - extra
    return np.array(holding)


def normal_values(key, dims, scale, most, split=(), kind=jnp.bfloat16):
    values = jax.random.normal(key, dims, jnp.float32) * scale
    if len(split) > 0:
        values = shard_levels(key, dims, split, -0.22, 0.18) * values
    return jnp.clip(values, min=-most, max=most).astype(kind)


def setup_inputs(seed: int = 0, part: int = 0) -> dict:
    key_of = jax.random.split(jax.random.key(seed), 10)
    own_keys = jax.random.split(jax.random.fold_in(key_of[9], part), 10)
    tokens = normal_values(own_keys[0], (TOKENS, D), 1.0, 6.0, ((0, 16),))
    expert_ids_keys = jax.random.split(jax.random.fold_in(own_keys[1], 1), TOKENS // TOK_DEV)
    expert_ids_turns = jax.random.permutation(jax.random.fold_in(own_keys[1], 3), TOKENS // TOK_DEV)
    expert_ids = jax.vmap(lambda own, number: deal_out(jax.random.fold_in(own_keys[1], 2), own, number, TOK_DEV, EXPERTS, TOP, CAP, 1))(expert_ids_keys, expert_ids_turns).reshape((TOKENS, TOP))
    gate_fixed = place_ends(jax.random.randint(own_keys[2], (TOKENS, TOP), 1, 65536), jax.random.fold_in(own_keys[2], 1), 1, 65535).astype(jnp.int32)
    gate_q = draw_gate_q(jax.random.fold_in(key_of[9], 71), part)
    up_q = draw_up_q(jax.random.fold_in(key_of[9], 71), part)
    down_q = draw_down_q(jax.random.fold_in(key_of[9], 71), part)
    gate_scale = draw_gate_scale(jax.random.fold_in(key_of[9], 71), part)
    up_scale = draw_up_scale(jax.random.fold_in(key_of[9], 71), part)
    down_scale = draw_down_scale(jax.random.fold_in(key_of[9], 71), part)
    return dict(tokens=tokens, expert_ids=expert_ids, gate_fixed=gate_fixed, gate_q=gate_q, up_q=up_q, down_q=down_q, gate_scale=gate_scale, up_scale=up_scale, down_scale=down_scale)


def reference(tokens, expert_ids, gate_fixed, gate_q, up_q, down_q, gate_scale, up_scale, down_scale):
    splits = N_EXPERT // WINDOW
    piece_width = FF // splits
    row_limit = N_EXPERT * CAP
    highest = lax.Precision.HIGHEST
    fixed = gate_fixed.astype(jnp.float32)
    weight = fixed / jnp.sum(fixed, axis=1, keepdims=True)
    onehot = (expert_ids[:, :, None] == jnp.arange(EXPERTS, dtype=jnp.int32)[None, None, :])
    token_weight = jnp.sum(onehot.astype(jnp.float32) * weight[:, :, None], axis=1)
    chosen = jnp.any(onehot, axis=1)
    summed = jnp.zeros((TOKENS, D), jnp.float32)
    for which in range(WINDOW):
        row_index = jnp.nonzero(chosen[:, which], size=row_limit, fill_value=0)[0].astype(jnp.int32)
        is_valid = (jnp.arange(row_limit) < jnp.sum(chosen[:, which].astype(jnp.int32))).astype(jnp.float32)
        routed_rows = tokens[row_index].astype(jnp.float32)
        lower = which * FF
        w_gate = gate_q[:, lower:lower + FF].astype(jnp.float32) * gate_scale[lower:lower + FF][None, :]
        w_up = up_q[:, lower:lower + FF].astype(jnp.float32) * up_scale[lower:lower + FF][None, :]
        gate_out = jnp.dot(routed_rows, w_gate, precision=highest)
        up_out = jnp.dot(routed_rows, w_up, precision=highest)
        hidden = (jax.nn.silu(gate_out) * up_out).astype(jnp.bfloat16)
        w_down = down_q[lower:lower + FF].astype(jnp.float32) * down_scale[which][None, :]
        pieces = jnp.einsum("rjf,jfd->rjd", hidden.astype(jnp.float32).reshape(row_limit, splits, piece_width),
                            w_down.reshape(splits, piece_width, D), precision=highest).astype(jnp.bfloat16)
        expert_out = jnp.sum(pieces.astype(jnp.float32), axis=1)
        row_scale = token_weight[row_index, which] * is_valid
        summed = summed.at[row_index].add(expert_out * row_scale[:, None])
    return summed.astype(jnp.bfloat16)
```

```python
import functools

import jax
import jax.numpy as jnp
from jax import lax
from jax.experimental import pallas as pl
from jax.experimental.pallas import tpu as pltpu
from jax.sharding import PartitionSpec as P

EXPERTS = 16
WINDOW = 8
CAP = 18


def expert_block(routed_rows, gate_q, up_q, down_q, gate_scale, up_scale, scale_row):
    gate_out = (
        jnp.dot(routed_rows, gate_q, preferred_element_type=jnp.float32) * gate_scale[None, :]
    )
    up_out = jnp.dot(routed_rows, up_q, preferred_element_type=jnp.float32) * up_scale[None, :]
    hidden = (jax.nn.silu(gate_out) * up_out).astype(jnp.bfloat16)
    partial_value = jnp.dot(hidden, down_q, preferred_element_type=jnp.float32) * scale_row
    return partial_value.astype(jnp.bfloat16)


def shards(tokens, expert_ids, gate_fixed, gate_q, up_q, down_q, gate_scale, up_scale, down_scale):
    devices = lax.axis_size("expert")
    splits = devices // WINDOW
    expert = lax.axis_index("expert") // splits
    width = tokens.shape[1]
    scale_row = lax.dynamic_slice_in_dim(down_scale, expert, 1, 0)
    experts_all = jnp.arange(EXPERTS, dtype=jnp.int32)
    slot_ids = jnp.arange(CAP, dtype=jnp.int32)
    onehot = expert_ids[:, :, None] == experts_all[None, None, :]
    chosen = jnp.any(onehot, axis=1).astype(jnp.int32)[:, :WINDOW]
    rank_in = jnp.cumsum(chosen, axis=0) - chosen
    placing = (chosen.T[:, None, :] == 1) & (rank_in.T[:, None, :] == slot_ids[None, :, None])
    outgoing = jnp.einsum(
        "ect,td->ecd", placing.astype(jnp.bfloat16), tokens, preferred_element_type=jnp.float32
    ).astype(jnp.bfloat16)
    outgoing = jnp.broadcast_to(outgoing[:, None], (WINDOW, splits, CAP, width)).reshape(
        devices, CAP, width
    )
    received = lax.all_to_all(outgoing, "expert", split_axis=0, concat_axis=0, tiled=True)
    slot_count = received.shape[1]
    flat_rows = received.reshape(devices * slot_count, width)
    partial_value = expert_block(flat_rows, gate_q, up_q, down_q, gate_scale, up_scale, scale_row)
    returned = lax.all_to_all(
        partial_value.reshape(devices, slot_count, width),
        "expert",
        split_axis=0,
        concat_axis=0,
        tiled=True,
    )
    expert_out = jnp.sum(returned.astype(jnp.float32).reshape(WINDOW, splits, CAP, width), axis=1)
    fixed = gate_fixed.astype(jnp.float32)
    weight = fixed / jnp.sum(fixed, axis=1, keepdims=True)
    token_weight = jnp.sum(onehot.astype(jnp.float32) * weight[:, :, None], axis=1)[:, :WINDOW]
    combining = placing.astype(jnp.float32) * token_weight.T[:, None, :]
    mixed = jnp.einsum("ect,ecd->td", combining, expert_out, precision=lax.Precision.HIGHEST)
    return mixed.astype(jnp.bfloat16)


MESH = pl.DeviceIdType.MESH
BASE = 16
OVER = CAP - BASE
CHIPS = WINDOW
ROWS = CHIPS * BASE
HALF = ROWS + CHIPS * OVER
LANES = 128
PIECES = BASE // OVER
CHUNK = PIECES * LANES
WIDE = CHUNK + LANES
TILE = 512


def iota(shape, dim):
    return lax.broadcasted_iota(jnp.int32, shape, dim)


def fused_kernel(
    tokens, ids, fixed, gate_w, up_w, down_w, gate_scale, up_scale, down_scale, out,
    wg, wu, wd, recv, send, back, acc_g, acc_u, hidden, sib,
    w_sem, d_sem, send_sem, recv_sem, fwd_send, fwd_recv, sib_send, sib_recv, back_send, back_recv,
):
    me = lax.axis_index("expert")
    chip = me // 2
    core = me % 2
    sibling = chip * 2 + 1 - core
    chunks = tokens.shape[1] // CHUNK
    units = wg.shape[2]
    toks = tokens.shape[0]

    def weight_copy(c, which):
        w, buf = ((gate_w, wg), (up_w, wu))[which]
        return pltpu.make_async_copy(w.at[pl.ds(c * CHUNK, CHUNK), :], buf.at[c], w_sem.at[c, which])

    def down_copy(d):
        return pltpu.make_async_copy(
            down_w.at[:, pl.ds(d * CHUNK, CHUNK)], wd.at[d % 2], d_sem.at[d % 2]
        )

    def peer(p):
        return ((chip + p) % CHIPS) * 2 + core

    mine = pl.multiple_of(core * HALF, 16)
    other = pl.multiple_of((1 - core) * HALF, 16)
    slot = pl.multiple_of(chip * BASE, 16)

    barrier = pltpu.get_barrier_semaphore()
    pl.semaphore_signal(barrier, inc=1, device_id={"expert": sibling}, device_id_type=MESH)
    for p in range(1, CHIPS):
        pl.semaphore_signal(barrier, inc=1, device_id={"expert": peer(p)}, device_id_type=MESH)

    for c in range(chunks):
        weight_copy(c, 0).start()
        weight_copy(c, 1).start()
    for d in range(2):
        down_copy(d).start()

    lane = iota((toks, LANES), 1)
    chosen = jnp.zeros((toks, LANES), jnp.float32)
    weight = jnp.zeros((toks, LANES), jnp.float32)
    fx = fixed[...].astype(jnp.float32)
    total = jnp.sum(fx, axis=1, keepdims=True)
    idv = ids[...]
    for k in range(idv.shape[1]):
        hit = (idv[:, k : k + 1] == lane // BASE).astype(jnp.float32)
        chosen = chosen + hit
        weight = weight + hit * (fx[:, k : k + 1] / total)
    before = (iota((toks, toks), 0) > iota((toks, toks), 1)).astype(jnp.bfloat16)
    rank = jnp.dot(before, chosen.astype(jnp.bfloat16), preferred_element_type=jnp.float32)
    main_t = jnp.where(rank == (lane % BASE).astype(jnp.float32), chosen, 0.0)
    over_t = jnp.where(rank == (BASE + lane % OVER).astype(jnp.float32), chosen, 0.0)
    piece_of = (lane % BASE) // OVER
    over_pieces = [jnp.where(piece_of == j, over_t, 0.0) for j in range(PIECES)]
    place_main = jnp.transpose(main_t).astype(jnp.bfloat16)
    place_over = jnp.transpose(jnp.concatenate(over_pieces, axis=0)).astype(jnp.bfloat16)

    def split(v):
        hi = v.astype(jnp.bfloat16)
        return [hi, (v - hi.astype(jnp.float32)).astype(jnp.bfloat16)]

    def gather(c):
        block = tokens[:, c * CHUNK : (c + 1) * CHUNK]
        send[c, :, :CHUNK] = jnp.dot(
            place_main, block, preferred_element_type=jnp.float32
        ).astype(jnp.bfloat16)
        stacked = jnp.concatenate(
            [block[:, j * LANES : (j + 1) * LANES] for j in range(PIECES)], axis=0
        )
        send[c, :, CHUNK:] = jnp.dot(
            place_over, stacked, preferred_element_type=jnp.float32
        ).astype(jnp.bfloat16)

    def dispatch(c, p):
        to = (chip + p) % CHIPS
        return pltpu.make_async_remote_copy(
            src_ref=send.at[c, pl.ds(pl.multiple_of(to * BASE, 16), BASE), :],
            dst_ref=recv.at[c, pl.ds(pl.multiple_of(mine + slot, 16), BASE), :],
            send_sem=send_sem.at[c, p],
            recv_sem=recv_sem.at[c, p],
            device_id={"expert": peer(p)},
            device_id_type=MESH,
        )

    def forward(c):
        return pltpu.make_async_remote_copy(
            src_ref=recv.at[c, pl.ds(mine, ROWS), :],
            dst_ref=recv.at[c, pl.ds(mine, ROWS), :],
            send_sem=fwd_send.at[c],
            recv_sem=fwd_recv.at[c],
            device_id={"expert": sibling},
            device_id_type=MESH,
        )

    def to_sibling(d):
        return pltpu.make_async_remote_copy(
            src_ref=recv.at[d, pl.ds(other, HALF), pl.ds(0, CHUNK)],
            dst_ref=sib.at[d],
            send_sem=sib_send.at[d],
            recv_sem=sib_recv.at[d],
            device_id={"expert": sibling},
            device_id_type=MESH,
        )

    def give_back(d, p):
        to = (chip + p) % CHIPS
        return pltpu.make_async_remote_copy(
            src_ref=send.at[d, pl.ds(pl.multiple_of(to * BASE, 16), BASE), :],
            dst_ref=back.at[d, pl.ds(slot, BASE), :],
            send_sem=back_send.at[d, p],
            recv_sem=back_recv.at[d, p],
            device_id={"expert": peer(p)},
            device_id_type=MESH,
        )

    gather(0)
    pl.semaphore_wait(barrier, CHIPS)
    for c in range(chunks):
        if c > 0:
            gather(c)
        for p in range(1, CHIPS):
            dispatch(c, p).start()
        recv[c, pl.ds(pl.multiple_of(mine + slot, 16), BASE), :] = send[c, pl.ds(slot, BASE), :]

    n_over = CHIPS * OVER
    r = iota((PIECES * n_over, ROWS), 0)
    q = iota((PIECES * n_over, ROWS), 1)
    unpack = (
        q == ((r % n_over) // OVER) * BASE + (r // n_over) * OVER + r % OVER
    ).astype(jnp.bfloat16)
    rt = iota((ROWS, PIECES * n_over), 1)
    qt = iota((ROWS, PIECES * n_over), 0)
    pack = (
        qt == ((rt % n_over) // OVER) * BASE + (rt // n_over) * OVER + rt % OVER
    ).astype(jnp.bfloat16)

    def columns(body):
        whole = units // TILE

        @pl.loop(0, whole)
        def _(n):
            body(pl.ds(pl.multiple_of(n * TILE, TILE), TILE))

        if units % TILE:
            body(pl.ds(whole * TILE, units % TILE))

    for c in range(chunks):
        for p in range(1, CHIPS):
            dispatch(c, p).wait_recv()
        forward(c).start()
        weight_copy(c, 0).wait()
        weight_copy(c, 1).wait()
        forward(c).wait_recv()
        for h in range(2):
            spread = jnp.dot(
                unpack, recv[c, h * HALF : h * HALF + ROWS, CHUNK:], preferred_element_type=jnp.float32
            ).astype(jnp.bfloat16)
            for j in range(PIECES):
                recv[c, h * HALF + ROWS : (h + 1) * HALF, j * LANES : (j + 1) * LANES] = spread[
                    j * n_over : (j + 1) * n_over
                ]

        def body(cols, c=c):
            x = recv[c, :, :CHUNK]
            g = jnp.dot(x, wg[c, :, cols], preferred_element_type=jnp.float32)
            u = jnp.dot(x, wu[c, :, cols], preferred_element_type=jnp.float32)
            if c > 0:
                g = g + acc_g[:, cols]
                u = u + acc_u[:, cols]
            if c < chunks - 1:
                acc_g[:, cols] = g
                acc_u[:, cols] = u
            else:
                g = g * gate_scale[:, cols]
                u = u * up_scale[:, cols]
                hidden[:, cols] = (g / (1.0 + jnp.exp(-g)) * u).astype(jnp.bfloat16)

        columns(body)

    for c in range(chunks):
        forward(c).wait_send()
        for p in range(1, CHIPS):
            dispatch(c, p).wait_send()

    def multiply_down(d):
        down_copy(d).wait()
        for t in range(CHUNK // TILE):
            piece = jnp.dot(
                hidden[...], wd[d % 2, :, t * TILE : (t + 1) * TILE], preferred_element_type=jnp.float32
            )
            lo = d * CHUNK + t * TILE
            piece = piece * down_scale[pl.ds(chip, 1), lo : lo + TILE]
            recv[d, :, t * TILE : (t + 1) * TILE] = piece.astype(jnp.bfloat16)
        to_sibling(d).start()
        if d + 2 < chunks:
            down_copy(d + 2).start()

    def finish(d):
        to_sibling(d).wait_recv()
        both = recv[d, pl.ds(mine, HALF), :CHUNK].astype(jnp.float32) + sib[d].astype(jnp.float32)
        both = both.astype(jnp.bfloat16)
        send[d, :, :CHUNK] = both[:ROWS]
        stacked = jnp.concatenate(
            [both[ROWS:, j * LANES : (j + 1) * LANES] for j in range(PIECES)], axis=0
        )
        send[d, :, CHUNK:] = jnp.dot(pack, stacked, preferred_element_type=jnp.float32).astype(
            jnp.bfloat16
        )
        for p in range(1, CHIPS):
            give_back(d, p).start()
        back[d, pl.ds(slot, BASE), :] = send[d, pl.ds(slot, BASE), :]

    for d in range(chunks):
        multiply_down(d)
        if d > 0:
            finish(d - 1)
    finish(chunks - 1)

    mix_main = jnp.concatenate(split(main_t * weight), axis=0)
    mix_over = jnp.concatenate(
        [part for j in range(PIECES) for part in split(over_pieces[j] * weight)], axis=0
    )
    for d in range(chunks):
        for p in range(1, CHIPS):
            give_back(d, p).wait_recv()
        main = jnp.dot(mix_main, back[d, :, :CHUNK], preferred_element_type=jnp.float32)
        main = main[:toks] + main[toks:]
        over = jnp.dot(mix_over, back[d, :, CHUNK:], preferred_element_type=jnp.float32)
        for j in range(PIECES):
            part = over[2 * j * toks : (2 * j + 1) * toks] + over[(2 * j + 1) * toks : (2 * j + 2) * toks]
            lo = d * CHUNK + j * LANES
            out[:, lo : lo + LANES] = (main[:, j * LANES : (j + 1) * LANES] + part).astype(jnp.bfloat16)

    for d in range(chunks):
        to_sibling(d).wait_send()
        for p in range(1, CHIPS):
            give_back(d, p).wait_send()


def fused_shards(tokens, expert_ids, gate_fixed, gate_q, up_q, down_q, gate_scale, up_scale, down_scale):
    toks, width = tokens.shape
    units = gate_q.shape[1]
    chunks = width // CHUNK
    bf16, f32 = jnp.bfloat16, jnp.float32
    vmem = pl.BlockSpec(memory_space=pltpu.VMEM)
    hbm = pl.BlockSpec(memory_space=pl.ANY)
    dma = pltpu.SemaphoreType.DMA
    return pl.pallas_call(
        fused_kernel,
        out_shape=jax.ShapeDtypeStruct((toks, width), bf16),
        in_specs=[vmem, vmem, vmem, hbm, hbm, hbm, vmem, vmem, vmem],
        out_specs=vmem,
        scratch_shapes=[
            pltpu.VMEM((chunks, CHUNK, units), bf16),
            pltpu.VMEM((chunks, CHUNK, units), bf16),
            pltpu.VMEM((2, units, CHUNK), bf16),
            pltpu.VMEM((chunks, 2 * HALF, WIDE), bf16),
            pltpu.VMEM((chunks, ROWS, WIDE), bf16),
            pltpu.VMEM((chunks, ROWS, WIDE), bf16),
            pltpu.VMEM((2 * HALF, units), f32),
            pltpu.VMEM((2 * HALF, units), f32),
            pltpu.VMEM((2 * HALF, units), bf16),
            pltpu.VMEM((chunks, HALF, CHUNK), bf16),
            dma((chunks, 2)),
            dma((2,)),
            dma((chunks, CHIPS)),
            dma((chunks, CHIPS)),
            dma((chunks,)),
            dma((chunks,)),
            dma((chunks,)),
            dma((chunks,)),
            dma((chunks, CHIPS)),
            dma((chunks, CHIPS)),
        ],
        compiler_params=pltpu.CompilerParams(
            collective_id=0, has_side_effects=True, vmem_limit_bytes=63 * 1024 * 1024
        ),
        cost_estimate=pl.CostEstimate(
            flops=12 * HALF * width * units, bytes_accessed=6 * width * units, transcendentals=2 * HALF * units
        ),
    )(
        tokens, expert_ids, gate_fixed, gate_q, up_q, down_q,
        gate_scale.reshape(1, units), up_scale.reshape(1, units), down_scale,
    )


def solution(mesh):
    placed = (
        P(("group", "expert"), None),
        P(("group", "expert"), None),
        P(("group", "expert"), None),
        P(None, "expert"),
        P(None, "expert"),
        P("expert", None),
        P("expert"),
        P("expert"),
        P(),
    )
    body = fused_shards if mesh.shape["expert"] == 2 * WINDOW else shards
    return jax.shard_map(
        body, mesh=mesh, in_specs=placed, out_specs=P(("group", "expert"), None), check_vma=False
    )
```

```python
import functools

import jax
import jax.numpy as jnp
from jax import lax
from jax.experimental import pallas as pl
from jax.experimental.pallas import tpu as pltpu
from jax.sharding import PartitionSpec as P

EXPERTS = 16
WINDOW = 8
CAP = 18


def expert_block(routed_rows, gate_q, up_q, down_q, gate_scale, up_scale, scale_row):
    gate_out = (
        jnp.dot(routed_rows, gate_q, preferred_element_type=jnp.float32) * gate_scale[None, :]
    )
    up_out = jnp.dot(routed_rows, up_q, preferred_element_type=jnp.float32) * up_scale[None, :]
    hidden = (jax.nn.silu(gate_out) * up_out).astype(jnp.bfloat16)
    partial_value = jnp.dot(hidden, down_q, preferred_element_type=jnp.float32) * scale_row
    return partial_value.astype(jnp.bfloat16)


def shards(tokens, expert_ids, gate_fixed, gate_q, up_q, down_q, gate_scale, up_scale, down_scale):
    devices = lax.axis_size("expert")
    splits = devices // WINDOW
    expert = lax.axis_index("expert") // splits
    width = tokens.shape[1]
    scale_row = lax.dynamic_slice_in_dim(down_scale, expert, 1, 0)
    experts_all = jnp.arange(EXPERTS, dtype=jnp.int32)
    slot_ids = jnp.arange(CAP, dtype=jnp.int32)
    onehot = expert_ids[:, :, None] == experts_all[None, None, :]
    chosen = jnp.any(onehot, axis=1).astype(jnp.int32)[:, :WINDOW]
    rank_in = jnp.cumsum(chosen, axis=0) - chosen
    placing = (chosen.T[:, None, :] == 1) & (rank_in.T[:, None, :] == slot_ids[None, :, None])
    outgoing = jnp.einsum(
        "ect,td->ecd", placing.astype(jnp.bfloat16), tokens, preferred_element_type=jnp.float32
    ).astype(jnp.bfloat16)
    outgoing = jnp.broadcast_to(outgoing[:, None], (WINDOW, splits, CAP, width)).reshape(
        devices, CAP, width
    )
    received = lax.all_to_all(outgoing, "expert", split_axis=0, concat_axis=0, tiled=True)
    slot_count = received.shape[1]
    flat_rows = received.reshape(devices * slot_count, width)
    partial_value = expert_block(flat_rows, gate_q, up_q, down_q, gate_scale, up_scale, scale_row)
    returned = lax.all_to_all(
        partial_value.reshape(devices, slot_count, width),
        "expert",
        split_axis=0,
        concat_axis=0,
        tiled=True,
    )
    expert_out = jnp.sum(returned.astype(jnp.float32).reshape(WINDOW, splits, CAP, width), axis=1)
    fixed = gate_fixed.astype(jnp.float32)
    weight = fixed / jnp.sum(fixed, axis=1, keepdims=True)
    token_weight = jnp.sum(onehot.astype(jnp.float32) * weight[:, :, None], axis=1)[:, :WINDOW]
    combining = placing.astype(jnp.float32) * token_weight.T[:, None, :]
    mixed = jnp.einsum("ect,ecd->td", combining, expert_out, precision=lax.Precision.HIGHEST)
    return mixed.astype(jnp.bfloat16)


MESH = pl.DeviceIdType.MESH
BASE = 16
OVER = CAP - BASE
CHIPS = WINDOW
ROWS = CHIPS * BASE
HALF = ROWS + CHIPS * OVER
LANES = 128
PIECES = BASE // OVER
CHUNK = PIECES * LANES
WIDE = CHUNK + LANES
TILE = 512


def iota(shape, dim):
    return lax.broadcasted_iota(jnp.int32, shape, dim)


def fused_kernel(
    tokens, ids, fixed, gate_w, up_w, down_w, gate_scale, up_scale, down_scale, out,
    wg, wu, wd, recv, send, back, acc_g, acc_u, hidden, sib, row_g, row_u,
    w_sem, d_sem, send_sem, recv_sem, fwd_send, fwd_recv, sib_send, sib_recv, back_send, back_recv,
):
    me = lax.axis_index("expert")
    chip = me // 2
    core = me % 2
    sibling = chip * 2 + 1 - core
    chunks = tokens.shape[1] // CHUNK
    units = wg.shape[2]
    toks = tokens.shape[0]

    def weight_copy(c, which):
        w, buf = ((gate_w, wg), (up_w, wu))[which]
        return pltpu.make_async_copy(w.at[pl.ds(c * CHUNK, CHUNK), :], buf.at[c], w_sem.at[c, which])

    def down_copy(d):
        return pltpu.make_async_copy(
            down_w.at[:, pl.ds(d * CHUNK, CHUNK)], wd.at[d % 2], d_sem.at[d % 2]
        )

    def peer(p):
        return ((chip + p) % CHIPS) * 2 + core

    mine = pl.multiple_of(core * HALF, 16)
    other = pl.multiple_of((1 - core) * HALF, 16)
    slot = pl.multiple_of(chip * BASE, 16)

    barrier = pltpu.get_barrier_semaphore()
    pl.semaphore_signal(barrier, inc=1, device_id={"expert": sibling}, device_id_type=MESH)
    for p in range(1, CHIPS):
        pl.semaphore_signal(barrier, inc=1, device_id={"expert": peer(p)}, device_id_type=MESH)

    for c in range(chunks):
        weight_copy(c, 0).start()
        weight_copy(c, 1).start()
    for d in range(2):
        down_copy(d).start()

    row_g[...] = gate_scale[...].reshape(1, units)
    row_u[...] = up_scale[...].reshape(1, units)

    lane = iota((toks, LANES), 1)
    chosen = jnp.zeros((toks, LANES), jnp.float32)
    weight = jnp.zeros((toks, LANES), jnp.float32)
    fx = jnp.transpose(fixed[...].astype(jnp.float32))
    total = jnp.sum(fx, axis=1, keepdims=True)
    idv = jnp.transpose(ids[...].astype(jnp.float32))
    owner = (lane // BASE).astype(jnp.float32)
    for k in range(idv.shape[1]):
        hit = (idv[:, k : k + 1] == owner).astype(jnp.float32)
        chosen = chosen + hit
        weight = weight + hit * (fx[:, k : k + 1] / total)
    before = (iota((toks, toks), 0) > iota((toks, toks), 1)).astype(jnp.bfloat16)
    rank = jnp.dot(before, chosen.astype(jnp.bfloat16), preferred_element_type=jnp.float32)
    main_t = jnp.where(rank == (lane % BASE).astype(jnp.float32), chosen, 0.0)
    over_t = jnp.where(rank == (BASE + lane % OVER).astype(jnp.float32), chosen, 0.0)
    piece_of = (lane % BASE) // OVER
    over_pieces = [jnp.where(piece_of == j, over_t, 0.0) for j in range(PIECES)]
    place_main = jnp.transpose(main_t).astype(jnp.bfloat16)
    place_over = jnp.transpose(jnp.concatenate(over_pieces, axis=0)).astype(jnp.bfloat16)

    def split(v):
        hi = v.astype(jnp.bfloat16)
        return [hi, (v - hi.astype(jnp.float32)).astype(jnp.bfloat16)]

    def gather(c):
        block = tokens[:, c * CHUNK : (c + 1) * CHUNK]
        send[c, :, :CHUNK] = jnp.dot(
            place_main, block, preferred_element_type=jnp.float32
        ).astype(jnp.bfloat16)
        stacked = jnp.concatenate(
            [block[:, j * LANES : (j + 1) * LANES] for j in range(PIECES)], axis=0
        )
        send[c, :, CHUNK:] = jnp.dot(
            place_over, stacked, preferred_element_type=jnp.float32
        ).astype(jnp.bfloat16)

    def dispatch(c, p):
        to = (chip + p) % CHIPS
        return pltpu.make_async_remote_copy(
            src_ref=send.at[c, pl.ds(pl.multiple_of(to * BASE, 16), BASE), :],
            dst_ref=recv.at[c, pl.ds(pl.multiple_of(mine + slot, 16), BASE), :],
            send_sem=send_sem.at[c, p],
            recv_sem=recv_sem.at[c, p],
            device_id={"expert": peer(p)},
            device_id_type=MESH,
        )

    def forward(c):
        return pltpu.make_async_remote_copy(
            src_ref=recv.at[c, pl.ds(mine, ROWS), :],
            dst_ref=recv.at[c, pl.ds(mine, ROWS), :],
            send_sem=fwd_send.at[c],
            recv_sem=fwd_recv.at[c],
            device_id={"expert": sibling},
            device_id_type=MESH,
        )

    def to_sibling(d):
        return pltpu.make_async_remote_copy(
            src_ref=recv.at[d, pl.ds(other, HALF), pl.ds(0, CHUNK)],
            dst_ref=sib.at[d],
            send_sem=sib_send.at[d],
            recv_sem=sib_recv.at[d],
            device_id={"expert": sibling},
            device_id_type=MESH,
        )

    def give_back(d, p):
        to = (chip + p) % CHIPS
        return pltpu.make_async_remote_copy(
            src_ref=send.at[d, pl.ds(pl.multiple_of(to * BASE, 16), BASE), :],
            dst_ref=back.at[d, pl.ds(slot, BASE), :],
            send_sem=back_send.at[d, p],
            recv_sem=back_recv.at[d, p],
            device_id={"expert": peer(p)},
            device_id_type=MESH,
        )

    gather(0)
    pl.semaphore_wait(barrier, CHIPS)
    for c in range(chunks):
        if c > 0:
            gather(c)
        for p in range(1, CHIPS):
            dispatch(c, p).start()
        recv[c, pl.ds(pl.multiple_of(mine + slot, 16), BASE), :] = send[c, pl.ds(slot, BASE), :]

    n_over = CHIPS * OVER
    r = iota((PIECES * n_over, ROWS), 0)
    q = iota((PIECES * n_over, ROWS), 1)
    unpack = (
        q == ((r % n_over) // OVER) * BASE + (r // n_over) * OVER + r % OVER
    ).astype(jnp.bfloat16)
    rt = iota((ROWS, PIECES * n_over), 1)
    qt = iota((ROWS, PIECES * n_over), 0)
    pack = (
        qt == ((rt % n_over) // OVER) * BASE + (rt // n_over) * OVER + rt % OVER
    ).astype(jnp.bfloat16)

    def columns(body):
        whole = units // TILE

        @pl.loop(0, whole)
        def _(n):
            body(pl.ds(pl.multiple_of(n * TILE, TILE), TILE))

        if units % TILE:
            body(pl.ds(whole * TILE, units % TILE))

    for c in range(chunks):
        for p in range(1, CHIPS):
            dispatch(c, p).wait_recv()
        forward(c).start()
        weight_copy(c, 0).wait()
        weight_copy(c, 1).wait()
        forward(c).wait_recv()
        for h in range(2):
            spread = jnp.dot(
                unpack, recv[c, h * HALF : h * HALF + ROWS, CHUNK:], preferred_element_type=jnp.float32
            ).astype(jnp.bfloat16)
            for j in range(PIECES):
                recv[c, h * HALF + ROWS : (h + 1) * HALF, j * LANES : (j + 1) * LANES] = spread[
                    j * n_over : (j + 1) * n_over
                ]

        def body(cols, c=c):
            x = recv[c, :, :CHUNK]
            g = jnp.dot(x, wg[c, :, cols], preferred_element_type=jnp.float32)
            u = jnp.dot(x, wu[c, :, cols], preferred_element_type=jnp.float32)
            if c > 0:
                g = g + acc_g[:, cols]
                u = u + acc_u[:, cols]
            if c < chunks - 1:
                acc_g[:, cols] = g
                acc_u[:, cols] = u
            else:
                g = g * row_g[:, cols]
                u = u * row_u[:, cols]
                hidden[:, cols] = (g / (1.0 + jnp.exp(-g)) * u).astype(jnp.bfloat16)

        columns(body)

    for c in range(chunks):
        forward(c).wait_send()
        for p in range(1, CHIPS):
            dispatch(c, p).wait_send()

    def multiply_down(d):
        down_copy(d).wait()
        for t in range(CHUNK // TILE):
            piece = jnp.dot(
                hidden[...], wd[d % 2, :, t * TILE : (t + 1) * TILE], preferred_element_type=jnp.float32
            )
            lo = d * CHUNK + t * TILE
            piece = piece * down_scale[pl.ds(chip, 1), lo : lo + TILE]
            recv[d, :, t * TILE : (t + 1) * TILE] = piece.astype(jnp.bfloat16)
        to_sibling(d).start()
        if d + 2 < chunks:
            down_copy(d + 2).start()

    def finish(d):
        to_sibling(d).wait_recv()
        both = recv[d, pl.ds(mine, HALF), :CHUNK].astype(jnp.float32) + sib[d].astype(jnp.float32)
        both = both.astype(jnp.bfloat16)
        send[d, :, :CHUNK] = both[:ROWS]
        stacked = jnp.concatenate(
            [both[ROWS:, j * LANES : (j + 1) * LANES] for j in range(PIECES)], axis=0
        )
        send[d, :, CHUNK:] = jnp.dot(pack, stacked, preferred_element_type=jnp.float32).astype(
            jnp.bfloat16
        )
        for p in range(1, CHIPS):
            give_back(d, p).start()
        back[d, pl.ds(slot, BASE), :] = send[d, pl.ds(slot, BASE), :]

    for d in range(chunks):
        multiply_down(d)
        if d > 0:
            finish(d - 1)
    finish(chunks - 1)

    mix_main = jnp.concatenate(split(main_t * weight), axis=0)
    mix_over = jnp.concatenate(
        [part for j in range(PIECES) for part in split(over_pieces[j] * weight)], axis=0
    )
    for d in range(chunks):
        for p in range(1, CHIPS):
            give_back(d, p).wait_recv()
        main = jnp.dot(mix_main, back[d, :, :CHUNK], preferred_element_type=jnp.float32)
        main = main[:toks] + main[toks:]
        over = jnp.dot(mix_over, back[d, :, CHUNK:], preferred_element_type=jnp.float32)
        for j in range(PIECES):
            part = over[2 * j * toks : (2 * j + 1) * toks] + over[(2 * j + 1) * toks : (2 * j + 2) * toks]
            lo = d * CHUNK + j * LANES
            out[:, lo : lo + LANES] = (main[:, j * LANES : (j + 1) * LANES] + part).astype(jnp.bfloat16)

    for d in range(chunks):
        to_sibling(d).wait_send()
        for p in range(1, CHIPS):
            give_back(d, p).wait_send()


def fused_shards(tokens, expert_ids, gate_fixed, gate_q, up_q, down_q, gate_scale, up_scale, down_scale):
    toks, width = tokens.shape
    units = gate_q.shape[1]
    chunks = width // CHUNK
    bf16, f32 = jnp.bfloat16, jnp.float32
    vmem = pl.BlockSpec(memory_space=pltpu.VMEM)
    hbm = pl.BlockSpec(memory_space=pl.ANY)
    dma = pltpu.SemaphoreType.DMA
    return pl.pallas_call(
        fused_kernel,
        out_shape=jax.ShapeDtypeStruct((toks, width), bf16),
        in_specs=[vmem, vmem, vmem, hbm, hbm, hbm, vmem, vmem, vmem],
        out_specs=vmem,
        scratch_shapes=[
            pltpu.VMEM((chunks, CHUNK, units), bf16),
            pltpu.VMEM((chunks, CHUNK, units), bf16),
            pltpu.VMEM((2, units, CHUNK), bf16),
            pltpu.VMEM((chunks, 2 * HALF, WIDE), bf16),
            pltpu.VMEM((chunks, ROWS, WIDE), bf16),
            pltpu.VMEM((chunks, ROWS, WIDE), bf16),
            pltpu.VMEM((2 * HALF, units), f32),
            pltpu.VMEM((2 * HALF, units), f32),
            pltpu.VMEM((2 * HALF, units), bf16),
            pltpu.VMEM((chunks, HALF, CHUNK), bf16),
            pltpu.VMEM((1, units), f32),
            pltpu.VMEM((1, units), f32),
            dma((chunks, 2)),
            dma((2,)),
            dma((chunks, CHIPS)),
            dma((chunks, CHIPS)),
            dma((chunks,)),
            dma((chunks,)),
            dma((chunks,)),
            dma((chunks,)),
            dma((chunks, CHIPS)),
            dma((chunks, CHIPS)),
        ],
        compiler_params=pltpu.CompilerParams(
            collective_id=0, has_side_effects=True, vmem_limit_bytes=63 * 1024 * 1024
        ),
        cost_estimate=pl.CostEstimate(
            flops=12 * HALF * width * units, bytes_accessed=6 * width * units, transcendentals=2 * HALF * units
        ),
    )(
        tokens, expert_ids.T, gate_fixed.T, gate_q, up_q, down_q, gate_scale, up_scale, down_scale
    )


def solution(mesh):
    placed = (
        P(("group", "expert"), None),
        P(("group", "expert"), None),
        P(("group", "expert"), None),
        P(None, "expert"),
        P(None, "expert"),
        P("expert", None),
        P("expert"),
        P("expert"),
        P(),
    )
    body = fused_shards if mesh.shape["expert"] == 2 * WINDOW else shards
    return jax.shard_map(
        body, mesh=mesh, in_specs=placed, out_specs=P(("group", "expert"), None), check_vma=False
    )
```

```python
import functools

import jax
import jax.numpy as jnp
from jax import lax
from jax.experimental import pallas as pl
from jax.experimental.pallas import tpu as pltpu
from jax.sharding import PartitionSpec as P

EXPERTS = 16
WINDOW = 8
CAP = 18


def expert_block(routed_rows, gate_q, up_q, down_q, gate_scale, up_scale, scale_row):
    gate_out = (
        jnp.dot(routed_rows, gate_q, preferred_element_type=jnp.float32) * gate_scale[None, :]
    )
    up_out = jnp.dot(routed_rows, up_q, preferred_element_type=jnp.float32) * up_scale[None, :]
    hidden = (jax.nn.silu(gate_out) * up_out).astype(jnp.bfloat16)
    partial_value = jnp.dot(hidden, down_q, preferred_element_type=jnp.float32) * scale_row
    return partial_value.astype(jnp.bfloat16)


def shards(tokens, expert_ids, gate_fixed, gate_q, up_q, down_q, gate_scale, up_scale, down_scale):
    devices = lax.axis_size("expert")
    splits = devices // WINDOW
    expert = lax.axis_index("expert") // splits
    width = tokens.shape[1]
    scale_row = lax.dynamic_slice_in_dim(down_scale, expert, 1, 0)
    experts_all = jnp.arange(EXPERTS, dtype=jnp.int32)
    slot_ids = jnp.arange(CAP, dtype=jnp.int32)
    onehot = expert_ids[:, :, None] == experts_all[None, None, :]
    chosen = jnp.any(onehot, axis=1).astype(jnp.int32)[:, :WINDOW]
    rank_in = jnp.cumsum(chosen, axis=0) - chosen
    placing = (chosen.T[:, None, :] == 1) & (rank_in.T[:, None, :] == slot_ids[None, :, None])
    outgoing = jnp.einsum(
        "ect,td->ecd", placing.astype(jnp.bfloat16), tokens, preferred_element_type=jnp.float32
    ).astype(jnp.bfloat16)
    outgoing = jnp.broadcast_to(outgoing[:, None], (WINDOW, splits, CAP, width)).reshape(
        devices, CAP, width
    )
    received = lax.all_to_all(outgoing, "expert", split_axis=0, concat_axis=0, tiled=True)
    slot_count = received.shape[1]
    flat_rows = received.reshape(devices * slot_count, width)
    partial_value = expert_block(flat_rows, gate_q, up_q, down_q, gate_scale, up_scale, scale_row)
    returned = lax.all_to_all(
        partial_value.reshape(devices, slot_count, width),
        "expert",
        split_axis=0,
        concat_axis=0,
        tiled=True,
    )
    expert_out = jnp.sum(returned.astype(jnp.float32).reshape(WINDOW, splits, CAP, width), axis=1)
    fixed = gate_fixed.astype(jnp.float32)
    weight = fixed / jnp.sum(fixed, axis=1, keepdims=True)
    token_weight = jnp.sum(onehot.astype(jnp.float32) * weight[:, :, None], axis=1)[:, :WINDOW]
    combining = placing.astype(jnp.float32) * token_weight.T[:, None, :]
    mixed = jnp.einsum("ect,ecd->td", combining, expert_out, precision=lax.Precision.HIGHEST)
    return mixed.astype(jnp.bfloat16)


MESH = pl.DeviceIdType.MESH
BASE = 16
OVER = CAP - BASE
CHIPS = WINDOW
ROWS = CHIPS * BASE
HALF = ROWS + CHIPS * OVER
LANES = 128
PIECES = BASE // OVER
CHUNK = PIECES * LANES
WIDE = CHUNK + LANES
TILE = 512


def iota(shape, dim):
    return lax.broadcasted_iota(jnp.int32, shape, dim)


def fused_kernel(
    tokens, ids, fixed, gate_w, up_w, down_w, gate_scale, up_scale, down_scale, out,
    wg, wu, wd, recv, send, back, acc_g, acc_u, hidden, sib, row_g, row_u,
    w_sem, d_sem, send_sem, recv_sem, fwd_send, fwd_recv, sib_send, sib_recv, back_send, back_recv,
):
    me = lax.axis_index("expert")
    chip = me // 2
    core = me % 2
    sibling = chip * 2 + 1 - core
    chunks = tokens.shape[1] // CHUNK
    units = wg.shape[2]
    toks = tokens.shape[0]

    def weight_copy(c, which):
        w, buf = ((gate_w, wg), (up_w, wu))[which]
        return pltpu.make_async_copy(w.at[pl.ds(c * CHUNK, CHUNK), :], buf.at[c], w_sem.at[c, which])

    def down_copy(d):
        return pltpu.make_async_copy(
            down_w.at[:, pl.ds(d * CHUNK, CHUNK)], wd.at[d % 2], d_sem.at[d % 2]
        )

    def peer(p):
        return ((chip + p) % CHIPS) * 2 + core

    mine = pl.multiple_of(core * HALF, 16)
    other = pl.multiple_of((1 - core) * HALF, 16)
    slot = pl.multiple_of(chip * BASE, 16)

    barrier = pltpu.get_barrier_semaphore()
    pl.semaphore_signal(barrier, inc=1, device_id={"expert": sibling}, device_id_type=MESH)
    for p in range(1, CHIPS):
        pl.semaphore_signal(barrier, inc=1, device_id={"expert": peer(p)}, device_id_type=MESH)

    for c in range(chunks):
        weight_copy(c, 0).start()
        weight_copy(c, 1).start()
    for d in range(2):
        down_copy(d).start()

    row_g[...] = gate_scale[...].reshape(1, units)
    row_u[...] = up_scale[...].reshape(1, units)

    lane = iota((toks, LANES), 1)
    chosen = jnp.zeros((toks, LANES), jnp.float32)
    weight = jnp.zeros((toks, LANES), jnp.float32)
    fx = jnp.transpose(fixed[...].astype(jnp.float32))
    total = jnp.sum(fx, axis=1, keepdims=True)
    idv = jnp.transpose(ids[...].astype(jnp.float32))
    owner = (lane // BASE).astype(jnp.float32)
    for k in range(idv.shape[1]):
        hit = (idv[:, k : k + 1] == owner).astype(jnp.float32)
        chosen = chosen + hit
        weight = weight + hit * (fx[:, k : k + 1] / total)
    before = (iota((toks, toks), 0) > iota((toks, toks), 1)).astype(jnp.bfloat16)
    rank = jnp.dot(before, chosen.astype(jnp.bfloat16), preferred_element_type=jnp.float32)
    main_t = jnp.where(rank == (lane % BASE).astype(jnp.float32), chosen, 0.0)
    over_t = jnp.where(rank == (BASE + lane % OVER).astype(jnp.float32), chosen, 0.0)
    piece_of = (lane % BASE) // OVER
    over_pieces = [jnp.where(piece_of == j, over_t, 0.0) for j in range(PIECES)]
    place_main = jnp.transpose(main_t).astype(jnp.bfloat16)
    place_over = jnp.transpose(jnp.concatenate(over_pieces, axis=0)).astype(jnp.bfloat16)

    def split(v):
        hi = v.astype(jnp.bfloat16)
        return [hi, (v - hi.astype(jnp.float32)).astype(jnp.bfloat16)]

    def gather(c):
        block = tokens[:, c * CHUNK : (c + 1) * CHUNK]
        send[c, :, :CHUNK] = jnp.dot(
            place_main, block, preferred_element_type=jnp.float32
        ).astype(jnp.bfloat16)
        stacked = jnp.concatenate(
            [block[:, j * LANES : (j + 1) * LANES] for j in range(PIECES)], axis=0
        )
        send[c, :, CHUNK:] = jnp.dot(
            place_over, stacked, preferred_element_type=jnp.float32
        ).astype(jnp.bfloat16)

    def dispatch(c, p):
        to = (chip + p) % CHIPS
        return pltpu.make_async_remote_copy(
            src_ref=send.at[c, pl.ds(pl.multiple_of(to * BASE, 16), BASE), :],
            dst_ref=recv.at[c, pl.ds(pl.multiple_of(mine + slot, 16), BASE), :],
            send_sem=send_sem.at[c, p],
            recv_sem=recv_sem.at[c, p],
            device_id={"expert": peer(p)},
            device_id_type=MESH,
        )

    def forward(c):
        return pltpu.make_async_remote_copy(
            src_ref=recv.at[c, pl.ds(mine, ROWS), :],
            dst_ref=recv.at[c, pl.ds(mine, ROWS), :],
            send_sem=fwd_send.at[c],
            recv_sem=fwd_recv.at[c],
            device_id={"expert": sibling},
            device_id_type=MESH,
        )

    def to_sibling(d):
        return pltpu.make_async_remote_copy(
            src_ref=recv.at[d, pl.ds(other, HALF), pl.ds(0, CHUNK)],
            dst_ref=sib.at[d],
            send_sem=sib_send.at[d],
            recv_sem=sib_recv.at[d],
            device_id={"expert": sibling},
            device_id_type=MESH,
        )

    def give_back(d, p):
        to = (chip + p) % CHIPS
        return pltpu.make_async_remote_copy(
            src_ref=send.at[d, pl.ds(pl.multiple_of(to * BASE, 16), BASE), :],
            dst_ref=back.at[d, pl.ds(slot, BASE), :],
            send_sem=back_send.at[d, p],
            recv_sem=back_recv.at[d, p],
            device_id={"expert": peer(p)},
            device_id_type=MESH,
        )

    gather(0)
    pl.semaphore_wait(barrier, CHIPS)
    for c in range(chunks):
        if c > 0:
            gather(c)
        for p in range(1, CHIPS):
            dispatch(c, p).start()
        recv[c, pl.ds(pl.multiple_of(mine + slot, 16), BASE), :] = send[c, pl.ds(slot, BASE), :]

    n_over = CHIPS * OVER
    r = iota((PIECES * n_over, ROWS), 0)
    q = iota((PIECES * n_over, ROWS), 1)
    unpack = (
        q == ((r % n_over) // OVER) * BASE + (r // n_over) * OVER + r % OVER
    ).astype(jnp.bfloat16)
    rt = iota((ROWS, PIECES * n_over), 1)
    qt = iota((ROWS, PIECES * n_over), 0)
    pack = (
        qt == ((rt % n_over) // OVER) * BASE + (rt // n_over) * OVER + rt % OVER
    ).astype(jnp.bfloat16)

    def columns(body):
        whole = units // TILE

        @pl.loop(0, whole)
        def _(n):
            body(pl.ds(pl.multiple_of(n * TILE, TILE), TILE))

        if units % TILE:
            body(pl.ds(whole * TILE, units % TILE))

    for c in range(chunks):
        for p in range(1, CHIPS):
            dispatch(c, p).wait_recv()
        forward(c).start()
        weight_copy(c, 0).wait()
        weight_copy(c, 1).wait()
        forward(c).wait_recv()
        for h in range(2):
            spread = jnp.dot(
                unpack, recv[c, h * HALF : h * HALF + ROWS, CHUNK:], preferred_element_type=jnp.float32
            ).astype(jnp.bfloat16)
            for j in range(PIECES):
                recv[c, h * HALF + ROWS : (h + 1) * HALF, j * LANES : (j + 1) * LANES] = spread[
                    j * n_over : (j + 1) * n_over
                ]

        def body(cols, c=c):
            x = recv[c, :, :CHUNK]
            g = jnp.dot(x, wg[c, :, cols], preferred_element_type=jnp.float32)
            u = jnp.dot(x, wu[c, :, cols], preferred_element_type=jnp.float32)
            if c > 0:
                g = g + acc_g[:, cols]
                u = u + acc_u[:, cols]
            if c < chunks - 1:
                acc_g[:, cols] = g
                acc_u[:, cols] = u
            else:
                g = g * row_g[:, cols]
                u = u * row_u[:, cols]
                hidden[:, cols] = (g / (1.0 + jnp.exp(-g)) * u).astype(jnp.bfloat16)

        columns(body)

    for c in range(chunks):
        forward(c).wait_send()
        for p in range(1, CHIPS):
            dispatch(c, p).wait_send()

    def multiply_down(d):
        down_copy(d).wait()
        for t in range(CHUNK // TILE):
            piece = jnp.dot(
                hidden[...], wd[d % 2, :, t * TILE : (t + 1) * TILE], preferred_element_type=jnp.float32
            )
            lo = d * CHUNK + t * TILE
            piece = piece * down_scale[pl.ds(chip, 1), lo : lo + TILE]
            recv[d, :, t * TILE : (t + 1) * TILE] = piece.astype(jnp.bfloat16)
            if t == 0 and d > 0:
                finish(d - 1)
        to_sibling(d).start()
        if d + 2 < chunks:
            down_copy(d + 2).start()

    def finish(d):
        to_sibling(d).wait_recv()
        both = recv[d, pl.ds(mine, HALF), :CHUNK].astype(jnp.float32) + sib[d].astype(jnp.float32)
        both = both.astype(jnp.bfloat16)
        send[d, :, :CHUNK] = both[:ROWS]
        stacked = jnp.concatenate(
            [both[ROWS:, j * LANES : (j + 1) * LANES] for j in range(PIECES)], axis=0
        )
        send[d, :, CHUNK:] = jnp.dot(pack, stacked, preferred_element_type=jnp.float32).astype(
            jnp.bfloat16
        )
        for p in range(1, CHIPS):
            give_back(d, p).start()
        back[d, pl.ds(slot, BASE), :] = send[d, pl.ds(slot, BASE), :]

    for d in range(chunks):
        multiply_down(d)
    finish(chunks - 1)

    mix_main = jnp.concatenate(split(main_t * weight), axis=0)
    mix_over = jnp.concatenate(
        [part for j in range(PIECES) for part in split(over_pieces[j] * weight)], axis=0
    )
    for d in range(chunks):
        for p in range(1, CHIPS):
            give_back(d, p).wait_recv()
        main = jnp.dot(mix_main, back[d, :, :CHUNK], preferred_element_type=jnp.float32)
        main = main[:toks] + main[toks:]
        over = jnp.dot(mix_over, back[d, :, CHUNK:], preferred_element_type=jnp.float32)
        for j in range(PIECES):
            part = over[2 * j * toks : (2 * j + 1) * toks] + over[(2 * j + 1) * toks : (2 * j + 2) * toks]
            lo = d * CHUNK + j * LANES
            out[:, lo : lo + LANES] = (main[:, j * LANES : (j + 1) * LANES] + part).astype(jnp.bfloat16)

    for d in range(chunks):
        to_sibling(d).wait_send()
        for p in range(1, CHIPS):
            give_back(d, p).wait_send()


def fused_shards(tokens, expert_ids, gate_fixed, gate_q, up_q, down_q, gate_scale, up_scale, down_scale):
    toks, width = tokens.shape
    units = gate_q.shape[1]
    chunks = width // CHUNK
    bf16, f32 = jnp.bfloat16, jnp.float32
    vmem = pl.BlockSpec(memory_space=pltpu.VMEM)
    hbm = pl.BlockSpec(memory_space=pl.ANY)
    dma = pltpu.SemaphoreType.DMA
    return pl.pallas_call(
        fused_kernel,
        out_shape=jax.ShapeDtypeStruct((toks, width), bf16),
        in_specs=[vmem, vmem, vmem, hbm, hbm, hbm, vmem, vmem, vmem],
        out_specs=vmem,
        scratch_shapes=[
            pltpu.VMEM((chunks, CHUNK, units), bf16),
            pltpu.VMEM((chunks, CHUNK, units), bf16),
            pltpu.VMEM((2, units, CHUNK), bf16),
            pltpu.VMEM((chunks, 2 * HALF, WIDE), bf16),
            pltpu.VMEM((chunks, ROWS, WIDE), bf16),
            pltpu.VMEM((chunks, ROWS, WIDE), bf16),
            pltpu.VMEM((2 * HALF, units), f32),
            pltpu.VMEM((2 * HALF, units), f32),
            pltpu.VMEM((2 * HALF, units), bf16),
            pltpu.VMEM((chunks, HALF, CHUNK), bf16),
            pltpu.VMEM((1, units), f32),
            pltpu.VMEM((1, units), f32),
            dma((chunks, 2)),
            dma((2,)),
            dma((chunks, CHIPS)),
            dma((chunks, CHIPS)),
            dma((chunks,)),
            dma((chunks,)),
            dma((chunks,)),
            dma((chunks,)),
            dma((chunks, CHIPS)),
            dma((chunks, CHIPS)),
        ],
        compiler_params=pltpu.CompilerParams(
            collective_id=0, has_side_effects=True, vmem_limit_bytes=63 * 1024 * 1024
        ),
        cost_estimate=pl.CostEstimate(
            flops=12 * HALF * width * units, bytes_accessed=6 * width * units, transcendentals=2 * HALF * units
        ),
    )(
        tokens, expert_ids.T, gate_fixed.T, gate_q, up_q, down_q, gate_scale, up_scale, down_scale
    )


def solution(mesh):
    placed = (
        P(("group", "expert"), None),
        P(("group", "expert"), None),
        P(("group", "expert"), None),
        P(None, "expert"),
        P(None, "expert"),
        P("expert", None),
        P("expert"),
        P("expert"),
        P(),
    )
    body = fused_shards if mesh.shape["expert"] == 2 * WINDOW else shards
    return jax.shard_map(
        body, mesh=mesh, in_specs=placed, out_specs=P(("group", "expert"), None), check_vma=False
    )
```
